512 devices in a mesh: dp: 4 (over x), tensor: 8 (over y), expert: 16 (over z, core).
Axes of the slice: x: 4, y: 8, z: 8, core: 2. Of those that a mesh axis runs over, the one named last changes fastest.
Arguments:
- tokens_a: bfloat16 [1024, 7168], P(('dp', 'expert')), may hold values from -6 to 6
- norm_gain: float32 [7168], replicated, may hold values from 0.25 to 1.75
- expert_ids: int32 [1024, 8], P(('dp', 'expert')), may hold values from 0 to 15, all different within a row; in each aligned block of 16 rows (0 to 15, 16 to 31, ...) at most 12 rows name the same one
- route_weights: float32 [1024, 8], P(('dp', 'expert')), may hold values from 0.1 to 0.5
- w_gate: bfloat16 [16, 7168, 2048], P('expert', 'dp', 'tensor'), may hold values from -0.0625 to 0.0625
- w_up: bfloat16 [16, 7168, 2048], P('expert', 'dp', 'tensor'), may hold values from -0.0625 to 0.0625
- w_down: bfloat16 [16, 2048, 7168], P('expert', 'tensor', 'dp'), may hold values from -0.125 to 0.125
- queries_b: bfloat16 [64, 16, 128, 576], P(('dp', 'expert'), None, 'tensor'), may hold values from -25 to 25
- cache_b: bfloat16 [64, 16, 256, 576], P(('dp', 'expert'), 'tensor'), may hold values from -1.6875 to 1.6875
- lengths_b: int32 [64, 16], P(('dp', 'expert'), 'tensor'), may hold values from 2 to 256
Outputs:
- mixed: bfloat16 [1024, 7168], P(('dp', 'expert'), 'tensor')
- latent_b: bfloat16 [64, 16, 128, 512], P(('dp', 'expert'), None, 'tensor')
The draws below stay inside these ranges and needn't reach their ends.
Inputs may be any that keep to these rules, and one draw needn't show every extreme that they name: `expert_ids`: each row names 8 different experts; among the 16 rows of one device no expert is named by more than 12 rows, a bound that some block reaches.
All inputs are finite; a program needn't handle non-finite values.
Results may differ from the reference program's by a relative error of at most 0.007.
Values may be sent and summed in bfloat16 or wider, within the bound.
No kernel may reach another device: no remote copies, remote signals or barrier semaphores. Data moves between devices by JAX's collectives and lax.ppermute only.
A program may use at most 64 MiB of HBM per device.

```python
import math
import jax
import jax.numpy as jnp
import numpy as np
from jax import lax

D = 7168
FF = 2048
H = 128
LAT = 512
ROPE = 64
ROWS_A = 16
ROWS_B = 16
CACHE = 256
EXPERTS = 16
TOP = 8
CAP = 12
NGROUP = 64
TOKENS_A = 1024
N_TENSOR = 8


def cache_base(key):
    return jax.random.uniform(key, (NGROUP, ROWS_B, CACHE, LAT + ROPE), jnp.float32, -1.6875, 1.6875)


def draw_cache_b(key, part):
    base = cache_base(key)
    return base.astype(jnp.bfloat16)


def draw_queries_b(key, part):
    key = jax.random.fold_in(key, 11)
    first_key = jax.random.fold_in(key, 0)
    shape = (NGROUP, ROWS_B, H, LAT + ROPE)
    values = jnp.clip(jax.random.normal(first_key, shape, jnp.float32), -6.0, 6.0)
    return values.astype(jnp.bfloat16)


def touch_ends(values, rng, least, largest):
    longest = values.shape.index(max(values.shape))
    spots = []
    for shift in (0, 1):
        where = [jax.random.randint(jax.random.fold_in(rng, axis), (), 0, length) for axis, length in enumerate(values.shape)]
        where[longest] = (where[longest] + shift) % values.shape[longest]
        spots.append(tuple(where))
    return values.at[spots[0]].set(least).at[spots[1]].set(largest)


def block_scale(stream_key, dims, cuts, smallest, largest):
    def one(position, parts):
        heights = jax.random.uniform(jax.random.fold_in(jax.random.fold_in(stream_key, 6), position), (parts,), jnp.float32, smallest / len(cuts), largest / len(cuts))
        return jnp.repeat(jnp.exp(heights), dims[position] // parts).reshape((-1,) + (1,) * (len(dims) - position - 1))

    factor_of = one(*cuts[0])
    for cut in cuts[1:]:
        factor_of = factor_of * one(*cut)
    return factor_of


def routed_block(key, own, number, rows, count, top, bound, skew):
    sequence = jax.random.permutation(key, count)
    packed, usual = load_shares(count, rows * top, bound, skew, True), load_shares(count, rows * top, bound, skew, False)
    places = jnp.arange(count)

    def named(sizes, turn):
        used = int((sizes > 0).sum())
        fixed = max(1, used // 4)
        moved = fixed + (places - fixed + turn * (used - fixed)) % max(1, count - fixed)
        return jnp.zeros((count,), jnp.int32).at[sequence[jnp.where(places < fixed, places, moved)]].set(jnp.asarray(sizes, jnp.int32))

    sizes = jnp.where(number % 4 == 0, named(packed, number // 4), named(usual, number - number // 4 - 1))
    mixed = jax.random.permutation(jax.random.fold_in(own, 3), count)
    giver, taker = mixed[0:count // 2 * 2:2], mixed[1:count // 2 * 2:2]
    room = jnp.minimum(sizes[giver] - 1, bound - sizes[taker]) // 2
    room = jnp.where((giver == sequence[0]) | (taker == sequence[0]) | (sizes[taker] == 0), 0, jnp.maximum(room, 0))
    moved = jax.random.randint(jax.random.fold_in(own, 4), (count // 2,), 0, 1 << 20) % (room + 1)
    sizes = sizes.at[giver].add(-moved).at[taker].add(moved)
    members = jnp.searchsorted(jnp.cumsum(sizes), jnp.arange(rows * top), side="right").astype(jnp.int32)
    table = members.reshape(top, rows).T
    table = table[jax.random.permutation(jax.random.fold_in(own, 1), rows)]
    turn = jax.random.randint(jax.random.fold_in(own, 2), (rows, 1), 0, top)
    return jnp.take_along_axis(table, (jnp.arange(top)[None, :] + turn) % top, axis=1)


def load_shares(count, total, bound, slope, full):
    weights = [(1 << 20) // math.isqrt(rank ** slope) + 1 for rank in range(1, count + 1)]
    largest = bound if full else min(bound, max(-(-total // count), total * weights[0] // sum(weights)))
    least = 1 if total - largest >= count - 1 else 0
    counts, spare = [largest] + [least] * (count - 1), total - largest - least * (count - 1)
    while spare > 0:
        candidates = [i for i in range(1, count) if counts[i] < largest] or [i for i in range(1, count) if counts[i] < bound]
        pool, left = sum([weights[i] for i in candidates]), spare
        for i in candidates:
            extra = min(bound - counts[i], max(1, left * weights[i] // pool), spare)
            counts[i] = counts[i] + extra
            spare = spare - extra
    return np.array(counts)


def scatter_about(stream_key, dims, spread, reach, shards=(), kind=jnp.bfloat16):
    result = spread * jax.random.normal(stream_key, dims, jnp.float32)
    if shards:
        result = result * block_scale(stream_key, dims, shards, -0.22, 0.18)
    return jnp.clip(result, -reach, reach).astype(kind)


def setup_inputs(seed: int = 0) -> dict:
    key_list = jax.random.split(jax.random.key(seed), 11)
    tokens_a = scatter_about(key_list[0], (TOKENS_A, D), 1.0, 6.0, ((0, 64),))
    norm_gain = jnp.clip(1.0 + 0.15 * jax.random.normal(key_list[1], (D,), jnp.float32), 0.25, 1.75)
    expert_ids_keys = jax.random.split(jax.random.fold_in(key_list[2], 1), TOKENS_A // ROWS_A)
    expert_ids_turns = jax.random.permutation(jax.random.fold_in(key_list[2], 3), TOKENS_A // ROWS_A)
    expert_ids = jax.vmap(lambda own, number: routed_block(jax.random.fold_in(key_list[2], 2), own, number, ROWS_A, EXPERTS, TOP, CAP, 2))(expert_ids_keys, expert_ids_turns).reshape((TOKENS_A, TOP))
    route_weights = jnp.clip(0.1 + 0.4 * jax.random.uniform(key_list[3], (TOKENS_A, TOP), jnp.float32) ** block_scale(key_list[3], (TOKENS_A, TOP), ((0, 64),), -0.2, 0.2), 0.1, 0.5)
    w_gate = scatter_about(key_list[4], (EXPERTS, D, FF), D ** -0.5, 0.0625, ((0, 16), (1, 4), (2, 8)))
    w_up = scatter_about(key_list[5], (EXPERTS, D, FF), D ** -0.5, 0.0625, ((0, 16), (1, 4), (2, 8)))
    w_down = scatter_about(key_list[6], (EXPERTS, FF, D), FF ** -0.5, 0.125, ((0, 16), (1, 8), (2, 4)))
    queries_b = draw_queries_b(jax.random.fold_in(key_list[10], 71), 0)
    cache_b = draw_cache_b(jax.random.fold_in(key_list[10], 71), 0)
    lengths_b = touch_ends(jax.random.randint(key_list[9], (NGROUP, ROWS_B), 2, CACHE + 1), jax.random.fold_in(key_list[9], 1), 2, CACHE).astype(jnp.int32)
    return {"tokens_a": tokens_a, "norm_gain": norm_gain, "expert_ids": expert_ids, "route_weights": route_weights, "w_gate": w_gate, "w_up": w_up, "w_down": w_down, "queries_b": queries_b, "cache_b": cache_b, "lengths_b": lengths_b}


score_scale = 192.0 ** (-0.5)

def norm_rows(tokens_a, norm_gain):
    values = tokens_a.astype(jnp.float32)
    row_scale = lax.rsqrt(lax.optimization_barrier(jnp.mean(values * values, axis=-1, keepdims=True)) + 1e-06)
    return (values * row_scale * norm_gain).astype(jnp.bfloat16)

def expert_output(normed, gate_w, up_w, down_w):
    gate_sum = jnp.dot(normed, gate_w, preferred_element_type=jnp.float32)
    up_sum = jnp.dot(normed, up_w, preferred_element_type=jnp.float32)
    active = (jax.nn.silu(gate_sum) * up_sum).astype(jnp.bfloat16)
    part_width = FF // N_TENSOR
    total_sum = jnp.zeros((normed.shape[0], D), jnp.float32)
    for block_idx in range(N_TENSOR):
        lower = block_idx * part_width
        down_piece = jnp.dot(active[:, lower:lower + part_width], down_w[lower:lower + part_width], preferred_element_type=jnp.float32)
        total_sum = total_sum + down_piece.astype(jnp.bfloat16).astype(jnp.float32)
    return total_sum

def one_group(inputs):
    queries, cache, lengths = inputs
    scores = jnp.einsum('rhc,rlc->rhl', queries.astype(jnp.float32), cache.astype(jnp.float32)) * score_scale
    live_mask = jnp.arange(CACHE, dtype=jnp.int32)[None, None, :] < lengths[:, None, None]
    scores = jnp.where(live_mask, scores, -1e+30)
    row_max = lax.optimization_barrier(jnp.max(scores, axis=-1, keepdims=True))
    exp_terms = jnp.exp(scores - row_max)
    softmax_bf = (exp_terms / lax.optimization_barrier(jnp.sum(exp_terms, axis=-1, keepdims=True))).astype(jnp.bfloat16)
    latent = jnp.einsum('rhl,rlc->rhc', softmax_bf.astype(jnp.float32), cache[:, :, :LAT].astype(jnp.float32))
    return latent.astype(jnp.bfloat16)

def reference(tokens_a, norm_gain, expert_ids, route_weights, w_gate, w_up, w_down, queries_b, cache_b, lengths_b):
    normed = norm_rows(tokens_a, norm_gain)

    def one_expert(running, expert_index):
        output = expert_output(normed, w_gate[expert_index], w_up[expert_index], w_down[expert_index])
        weight = lax.optimization_barrier(jnp.sum(jnp.where(expert_ids == expert_index, route_weights, jnp.zeros_like(route_weights)), axis=1))
        return (running + weight[:, None] * output, None)
    mixed_sum, unused = lax.scan(one_expert, jnp.zeros((TOKENS_A, D), jnp.float32), jnp.arange(EXPERTS, dtype=jnp.int32))
    latent_b = lax.map(one_group, (queries_b, cache_b, lengths_b))
    return (mixed_sum.astype(jnp.bfloat16), latent_b)
```

```python
import functools

import jax
import jax.numpy as jnp
from jax import lax
from jax.experimental import pallas as pl
from jax.experimental.pallas import tpu as pltpu
from jax.sharding import Mesh, PartitionSpec as P

LAT = 512
BF = jnp.bfloat16
F32 = jnp.float32
score_scale = 192.0 ** (-0.5)
VMEM = pl.BlockSpec(memory_space=pltpu.VMEM)
PARAMS = pltpu.CompilerParams(vmem_limit_bytes=48 * 1024 * 1024)


def norm_kernel(tokens_ref, gain_ref, out_ref):
    values = tokens_ref[...].astype(F32)
    row_scale = lax.rsqrt(jnp.mean(values * values, axis=-1, keepdims=True) + 1e-06)
    normed = (values * row_scale * gain_ref[...]).astype(BF)
    parts, _, width = out_ref.shape
    for part in range(parts):
        out_ref[part] = normed[:, part * width : (part + 1) * width]


def gate_up_kernel(rows_ref, gate_ref, up_ref, out_ref):
    z_count, cores, x_count, rows, width = rows_ref.shape
    me = lax.axis_index("c")
    flat = rows_ref[...].reshape(z_count * cores * x_count * rows, width)
    hidden = gate_ref.shape[1]
    for number, weight in enumerate((gate_ref, up_ref)):
        part = jnp.dot(flat, weight[...], preferred_element_type=F32).astype(BF)
        part = part.reshape(z_count, cores, x_count, rows, hidden)
        for core in range(cores):
            place = lax.rem(core + me, cores)
            for x in range(x_count):
                out_ref[x, place, :, :, number * hidden : (number + 1) * hidden] = part[:, core, x]


def active_kernel(parts_ref, out_ref):
    hidden = out_ref.shape[1]
    total = parts_ref[0].astype(F32)
    for x in range(1, parts_ref.shape[0]):
        total = total + parts_ref[x].astype(F32)
    gate, up = total[:, :hidden], total[:, hidden:]
    out_ref[...] = (gate / (1.0 + jnp.exp(-gate)) * up).astype(BF)


def down_kernel(mine_ref, other_ref, coef_ref, *refs):
    weights, (keep_ref, send_ref) = refs[:-2], refs[-2:]
    x_count = len(weights)
    me = lax.axis_index("x")
    half = keep_ref.shape[1]
    coef = coef_ref[...]
    for shift, weight in enumerate(weights):
        place = lax.rem(me + x_count - shift, x_count)
        first = jnp.dot(mine_ref[...], weight[0], preferred_element_type=F32).astype(BF).astype(F32)
        second = jnp.dot(other_ref[...], weight[1], preferred_element_type=F32).astype(BF).astype(F32)
        total = (first + second) * coef
        keep_ref[place] = total[:half]
        send_ref[place] = total[half:].astype(BF)


def attend(queries, cache, lengths):
    scores = (
        jnp.einsum("rhc,rlc->rhl", queries, cache, preferred_element_type=F32) * score_scale
    )
    live_mask = lax.broadcasted_iota(jnp.int32, scores.shape, 2) < lengths[:, None, None]
    scores = jnp.where(live_mask, scores, -1e30)
    row_max = jnp.max(scores, axis=2, keepdims=True)
    exp_terms = jnp.exp(scores - row_max)
    softmax_bf = (exp_terms / jnp.sum(exp_terms, axis=2, keepdims=True)).astype(BF)
    latent = jnp.einsum("rhl,rlc->rhc", softmax_bf, cache[:, :, :LAT], preferred_element_type=F32)
    return latent.astype(BF)


def attention(queries_b, cache_b, lengths_b):
    rows_b, heads_dev, channels = queries_b.shape[1:]
    tensor_size = lax.axis_size("k") * lax.axis_size("h")
    rows_owned = cache_b.shape[1]
    asked = queries_b[0].reshape(tensor_size, rows_owned, heads_dev, channels)
    pieces = lax.all_to_all(asked, ("k", "h"), split_axis=0, concat_axis=0, tiled=True)
    merged = pieces.transpose(1, 0, 2, 3).reshape(rows_owned, tensor_size * heads_dev, channels)
    result = attend(merged, cache_b[0], lengths_b[0])
    result = result.reshape(rows_owned, tensor_size, heads_dev, LAT).transpose(1, 0, 2, 3)
    answers = lax.all_to_all(result, ("k", "h"), split_axis=0, concat_axis=0, tiled=True)
    return answers.reshape(1, rows_b, heads_dev, LAT)


def swap(array, axis):
    return lax.ppermute(array, axis, [(0, 1), (1, 0)])


def shards(
    tokens_a,
    norm_gain,
    expert_ids,
    route_weights,
    w_gate,
    w_up,
    w_down,
    queries_b,
    cache_b,
    lengths_b,
):
    x_size, z_size, cores = lax.axis_size("x"), lax.axis_size("z"), lax.axis_size("c")
    rows = tokens_a.shape[0]
    width = w_gate.shape[1]
    hidden = w_gate.shape[2]
    experts = z_size * cores
    group_rows = experts * rows

    normed = pl.pallas_call(
        norm_kernel,
        out_shape=jax.ShapeDtypeStruct((x_size, rows, width), BF),
        in_specs=[VMEM, VMEM],
        out_specs=VMEM,
        compiler_params=PARAMS,
        name="norm_rows",
    )(tokens_a, norm_gain.reshape(1, -1))
    sliced = lax.all_to_all(normed, "x", split_axis=0, concat_axis=0, tiled=True)
    gathered = lax.all_gather(
        sliced.reshape(x_size * rows, width), ("z", "c"), axis=0, tiled=True
    ).reshape(z_size, cores, x_size, rows, width)

    side = lax.axis_index("h")
    columns = w_down.shape[2] // 2
    left, right = w_down[0][:, :columns], w_down[0][:, columns:]
    w_mine = jnp.where(side == 0, left, right)
    w_theirs = swap(jnp.where(side == 0, right, left), "h")
    w_pair = jnp.stack([w_mine, w_theirs])
    w_all = [w_pair] + [
        lax.ppermute(w_pair, "x", [(i, (i + s) % x_size) for i in range(x_size)])
        for s in range(1, x_size)
    ]

    chosen = expert_ids.T[None] == lax.broadcasted_iota(jnp.int32, (experts, 1, 1), 0)
    weight = jnp.sum(jnp.where(chosen, route_weights.T[None], 0.0), axis=1)
    coef = lax.all_to_all(weight, ("z", "c"), split_axis=0, concat_axis=0, tiled=True)
    coef = coef.reshape(z_size, cores, rows)
    core = lax.axis_index("c")
    coef = jnp.where(
        core == 0,
        jnp.stack([coef[:, 0], coef[:, 1]]),
        jnp.stack([coef[:, 1], coef[:, 0]]),
    ).reshape(group_rows, 1)

    latent_b = attention(queries_b, cache_b, lengths_b)

    steps = 2
    partial = pl.pallas_call(
        gate_up_kernel,
        grid=(steps,),
        out_shape=jax.ShapeDtypeStruct((x_size, cores, z_size, rows, 2 * hidden), BF),
        in_specs=[
            pl.BlockSpec((z_size // steps, cores, x_size, rows, width), lambda i: (i, 0, 0, 0, 0)),
            pl.BlockSpec((width, hidden), lambda i: (0, 0)),
            pl.BlockSpec((width, hidden), lambda i: (0, 0)),
        ],
        out_specs=pl.BlockSpec(
            (x_size, cores, z_size // steps, rows, 2 * hidden), lambda i: (0, 0, i, 0, 0)
        ),
        compiler_params=PARAMS,
        cost_estimate=pl.CostEstimate(
            flops=4 * x_size * group_rows * width * hidden,
            bytes_accessed=2 * x_size * group_rows * (width + 2 * hidden) + 4 * width * hidden,
            transcendentals=0,
        ),
        name="gate_up",
    )(gathered, w_gate[0], w_up[0])
    partial = partial.reshape(x_size, group_rows, 2 * hidden)
    parts = lax.all_to_all(partial, "x", split_axis=0, concat_axis=0, tiled=True)
    active = pl.pallas_call(
        active_kernel,
        out_shape=jax.ShapeDtypeStruct((group_rows, hidden), BF),
        in_specs=[VMEM],
        out_specs=VMEM,
        compiler_params=PARAMS,
        name="active_rows",
    )(parts)
    active_other = swap(active, "h")

    half = group_rows // cores
    keep, send = pl.pallas_call(
        down_kernel,
        out_shape=(
            jax.ShapeDtypeStruct((x_size, half, columns), F32),
            jax.ShapeDtypeStruct((x_size, half, columns), BF),
        ),
        in_specs=[VMEM] * (3 + x_size),
        out_specs=(VMEM, VMEM),
        compiler_params=PARAMS,
        name="down_rows",
    )(active, active_other, coef, *w_all)
    both = (keep + swap(send, "c").astype(F32)).astype(BF)
    by_y = lax.all_to_all(both, "k", split_axis=0, concat_axis=0, tiled=True)
    sum_y = jnp.sum(by_y.astype(F32), axis=0).astype(BF).reshape(z_size, rows, columns)
    by_z = lax.all_to_all(sum_y, "z", split_axis=0, concat_axis=0, tiled=True)
    mixed = jnp.sum(by_z.astype(F32), axis=0).astype(BF)
    return (mixed, latent_b)


def solution(mesh):
    x_size, y_size, e_size = (mesh.shape[name] for name in ("dp", "tensor", "expert"))
    cores = 2
    fine = Mesh(
        mesh.devices.reshape(x_size, y_size // 2, 2, e_size // cores, cores),
        ("x", "k", "h", "z", "c"),
    )
    rows, tensor, expert = ("x", "z", "c"), ("k", "h"), ("z", "c")
    placed = (
        P(rows, None),
        P(),
        P(rows, None),
        P(rows, None),
        P(expert, "x", tensor),
        P(expert, "x", tensor),
        P(expert, tensor, "x"),
        P(rows, None, tensor, None),
        P(rows, tensor, None, None),
        P(rows, tensor),
    )
    return jax.shard_map(
        shards,
        mesh=fine,
        in_specs=placed,
        out_specs=(P(rows, tensor), P(rows, None, tensor, None)),
        check_vma=False,
    )
```

```python
import functools

import jax
import jax.numpy as jnp
from jax import lax
from jax.experimental import pallas as pl
from jax.experimental.pallas import tpu as pltpu
from jax.sharding import Mesh, PartitionSpec as P

LAT = 512
BF = jnp.bfloat16
F32 = jnp.float32
score_scale = 192.0 ** (-0.5)
VMEM = pl.BlockSpec(memory_space=pltpu.VMEM)
PARAMS = pltpu.CompilerParams(vmem_limit_bytes=48 * 1024 * 1024)
WIDE = pltpu.CompilerParams(vmem_limit_bytes=60 * 1024 * 1024)


def norm_kernel(tokens_ref, gain_ref, ids_ref, route_ref, out_ref):
    values = tokens_ref[...].astype(F32)
    row_scale = lax.rsqrt(jnp.mean(values * values, axis=-1, keepdims=True) + 1e-06)
    normed = (values * row_scale * gain_ref[...]).astype(BF)
    parts, _, columns = out_ref.shape
    width = normed.shape[1] // parts
    experts = lax.axis_size("z") * lax.axis_size("c")
    ids, route = ids_ref[...], route_ref[...]
    table = jnp.concatenate(
        [
            jnp.sum(jnp.where(ids == expert, route, 0.0), axis=0, keepdims=True)
            for expert in range(experts)
        ],
        axis=0,
    )
    high = table.astype(BF)
    low = (table - high.astype(F32)).astype(BF)
    both = jnp.concatenate([high.astype(F32), low.astype(F32)], axis=0).astype(BF)
    shape = (2 * experts, columns - width)
    spread = lax.broadcasted_iota(jnp.int32, shape, 0) == lax.broadcasted_iota(jnp.int32, shape, 1)
    extra = lax.dot_general(
        both, spread.astype(F32).astype(BF), (((0,), (0,)), ((), ())), preferred_element_type=F32
    ).astype(BF)
    for part in range(parts):
        out_ref[part, :, :width] = normed[:, part * width : (part + 1) * width]
        out_ref[part, :, width:columns] = extra


def gate_up_kernel(rows_ref, gate_ref, up_ref, out_ref):
    z_count, cores, x_count, rows, width = rows_ref.shape
    me = lax.axis_index("c")
    flat = rows_ref[...].reshape(z_count * cores * x_count * rows, width)
    hidden = gate_ref.shape[1]
    for number, weight in enumerate((gate_ref, up_ref)):
        part = jnp.dot(flat, weight[...], preferred_element_type=F32).astype(BF)
        part = part.reshape(z_count, cores, x_count, rows, hidden)
        for core in range(cores):
            place = 1 - lax.rem(core + me, cores)
            for x in range(x_count):
                out_ref[x, place, :, :, number * hidden : (number + 1) * hidden] = part[:, core, x]


def active_kernel(parts_ref, out_ref):
    hidden = out_ref.shape[1]
    total = parts_ref[0].astype(F32)
    for x in range(1, parts_ref.shape[0]):
        total = total + parts_ref[x].astype(F32)
    gate, up = total[:, :hidden], total[:, hidden:]
    out_ref[...] = (gate / (1.0 + jnp.exp(-gate)) * up).astype(BF)


def down_kernel(place_ref, mine_ref, other_ref, route_ref, *refs):
    (pair_ref, lower_ref, upper_ref), across = refs[:3], refs[3:5]
    added, out_ref = refs[5:-1], refs[-1]
    weights = [ref.at[half] for ref in (pair_ref, lower_ref, upper_ref) for half in (0, 1)]
    weights += across
    x_count = out_ref.shape[0]
    me = lax.axis_index("x")
    rows = mine_ref.shape[0]
    route = route_ref[...].reshape(rows, route_ref.shape[-1]).astype(F32)
    lane = lax.broadcasted_iota(jnp.int32, route.shape, 1)
    experts = lax.axis_size("z") * lax.axis_size("c")
    own = lax.axis_index("z") * lax.axis_size("c") + lax.axis_index("c")
    hit = (lane == own) | (lane == own + experts)
    coef = jnp.sum(jnp.where(hit, route, 0.0), axis=1, keepdims=True)
    for step, number in ((0, 0), (3, 2), (1, 4), (2, 6)):
        place = lax.rem(me + step, x_count)
        first = jnp.dot(mine_ref[...], weights[number][...], preferred_element_type=F32)
        second = jnp.dot(other_ref[...], weights[number + 1][...], preferred_element_type=F32)
        total = (first.astype(BF).astype(F32) + second.astype(BF).astype(F32)) * coef
        for ref in added:
            total = total + ref[place].astype(F32)
        out_ref[place] = total.astype(BF)


def attend(queries, cache, lengths):
    scores = (
        jnp.einsum("rhc,rlc->rhl", queries, cache, preferred_element_type=F32) * score_scale
    )
    live_mask = lax.broadcasted_iota(jnp.int32, scores.shape, 2) < lengths[:, None, None]
    scores = jnp.where(live_mask, scores, -1e30)
    row_max = jnp.max(scores, axis=2, keepdims=True)
    exp_terms = jnp.exp(scores - row_max)
    softmax_bf = (exp_terms / jnp.sum(exp_terms, axis=2, keepdims=True)).astype(BF)
    latent = jnp.einsum("rhl,rlc->rhc", softmax_bf, cache[:, :, :LAT], preferred_element_type=F32)
    return latent.astype(BF)


def attention(queries_b, cache_b, lengths_b):
    heads_dev, channels = queries_b.shape[2:]
    tensor_size = lax.axis_size("k") * lax.axis_size("h")
    rows_owned = cache_b.shape[1]
    asked = queries_b[0].reshape(tensor_size, rows_owned, heads_dev, channels)
    pieces = lax.all_to_all(asked, ("k", "h"), split_axis=0, concat_axis=0, tiled=True)
    merged = pieces.transpose(1, 0, 2, 3).reshape(rows_owned, tensor_size * heads_dev, channels)
    result = attend(merged, cache_b[0], lengths_b[0])
    return result.reshape(rows_owned, tensor_size, heads_dev, LAT).transpose(1, 0, 2, 3)


def answer(result):
    answers = lax.all_to_all(result, ("k", "h"), split_axis=0, concat_axis=0, tiled=True)
    tensor_size, rows_owned, heads_dev, channels = answers.shape
    return answers.reshape(1, tensor_size * rows_owned, heads_dev, channels)


def swap(array, axis):
    return lax.ppermute(array, axis, [(0, 1), (1, 0)])


def shift(array, step):
    size = lax.axis_size("x")
    return lax.ppermute(array, "x", [(i, (i + step) % size) for i in range(size)])


def gate_up(gathered, w_gate, w_up):
    z_size, cores, x_size, rows, _ = gathered.shape
    width, hidden = w_gate.shape
    steps = 2
    partial = pl.pallas_call(
        gate_up_kernel,
        grid=(steps,),
        out_shape=jax.ShapeDtypeStruct((x_size, cores, z_size, rows, 2 * hidden), BF),
        in_specs=[
            pl.BlockSpec((z_size // steps, cores, x_size, rows, width), lambda i: (i, 0, 0, 0, 0)),
            pl.BlockSpec((width, hidden), lambda i: (0, 0)),
            pl.BlockSpec((width, hidden), lambda i: (0, 0)),
        ],
        out_specs=pl.BlockSpec(
            (x_size, cores, z_size // steps, rows, 2 * hidden), lambda i: (0, 0, i, 0, 0)
        ),
        compiler_params=WIDE,
        name="gate_up",
    )(gathered, w_gate, w_up)
    return partial.reshape(x_size, cores * z_size * rows, 2 * hidden)


def swiglu(parts):
    return pl.pallas_call(
        active_kernel,
        out_shape=jax.ShapeDtypeStruct((parts.shape[1], parts.shape[2] // 2), BF),
        in_specs=[VMEM],
        out_specs=VMEM,
        compiler_params=PARAMS,
        name="active_rows",
    )(parts)


def down(half, mine, other, gathered, place, weights, added):
    z_size, cores, x_size, rows, columns = gathered.shape
    count, hidden = mine.shape[0] // cores, mine.shape[1]
    lanes = 128
    last = columns // lanes - 1
    whole = pl.BlockSpec(memory_space=pltpu.VMEM)
    out_columns = weights[0].shape[2]
    return pl.pallas_call(
        down_kernel,
        out_shape=jax.ShapeDtypeStruct((x_size, count, out_columns), BF),
        grid_spec=pltpu.PrefetchScalarGridSpec(
            num_scalar_prefetch=1,
            grid=(1,),
            in_specs=[
                pl.BlockSpec((count, hidden), lambda i, p: (half, 0)),
                pl.BlockSpec((count, hidden), lambda i, p: (half, 0)),
                pl.BlockSpec((z_size, 1, 1, rows, lanes), lambda i, p: (0, p[0], p[1], 0, last)),
            ]
            + [whole] * (len(weights) + len(added)),
            out_specs=whole,
        ),
        compiler_params=PARAMS,
        name="down_rows",
    )(place, mine, other, gathered, *weights, *added)


def shards(
    tokens_a,
    norm_gain,
    expert_ids,
    route_weights,
    w_gate,
    w_up,
    w_down,
    queries_b,
    cache_b,
    lengths_b,
):
    x_size, z_size, cores = lax.axis_size("x"), lax.axis_size("z"), lax.axis_size("c")
    rows = tokens_a.shape[0]
    width = w_gate.shape[1]
    lanes = 128

    normed = pl.pallas_call(
        norm_kernel,
        grid=(1,),
        out_shape=jax.ShapeDtypeStruct((x_size, rows, width + lanes), BF),
        in_specs=[
            pl.BlockSpec(shape, lambda i: (0, 0))
            for shape in (tokens_a.shape, (1, norm_gain.shape[0])) + 2 * (expert_ids.shape[::-1],)
        ],
        out_specs=VMEM,
        compiler_params=WIDE,
        name="norm_rows",
    )(tokens_a, norm_gain.reshape(1, -1), expert_ids.T, route_weights.T)
    sliced = lax.all_to_all(normed, "x", split_axis=0, concat_axis=0, tiled=True)
    gathered = lax.all_gather(
        sliced.reshape(x_size * rows, width + lanes), ("z", "c"), axis=0, tiled=True
    ).reshape(z_size, cores, x_size, rows, width + lanes)

    normed, w_down = lax.optimization_barrier((normed, w_down))
    side = lax.axis_index("h")
    columns = w_down.shape[2] // 2
    left, right = w_down[0][:, :columns], w_down[0][:, columns:]
    mine = jnp.where(side == 0, left, right)
    theirs = swap(jnp.where(side == 0, right, left), "h")
    pair = jnp.stack([mine, theirs])
    lower, upper = shift(pair, 1), shift(pair, -1)
    across = (shift(lower[0], 1), shift(upper[1], -1))

    result = attention(queries_b, cache_b, lengths_b)
    latent_b = answer(result)
    gathered, latent_b, pair, lower, upper, across = lax.optimization_barrier(
        (gathered, latent_b, pair, lower, upper, across)
    )
    core, x_place = lax.axis_index("c"), lax.axis_index("x")
    partial = gate_up(gathered, w_gate[0], w_up[0])
    parts = lax.all_to_all(partial, "x", split_axis=0, concat_axis=0, tiled=True)
    weights = (pair, lower, upper, *across)
    active = swiglu(parts)
    active_other = swap(active, "h")
    added = ()
    for half in range(cores):
        place = jnp.stack([lax.rem(core + 1 + half, cores), x_place])
        out = down(half, active, active_other, gathered, place, weights, added)
        if not added:
            added = (swap(out, "c"),)
    both = out.reshape(-1, rows, columns)
    landed = lax.all_to_all(both, ("k", "z"), split_axis=0, concat_axis=0, tiled=True)
    mixed = jnp.sum(landed.astype(F32), axis=0).astype(BF)
    return (mixed, latent_b)


def solution(mesh):
    x_size, y_size, e_size = (mesh.shape[name] for name in ("dp", "tensor", "expert"))
    cores = 2
    fine = Mesh(
        mesh.devices.reshape(x_size, y_size // 2, 2, e_size // cores, cores),
        ("x", "k", "h", "z", "c"),
    )
    rows, tensor, expert = ("x", "z", "c"), ("k", "h"), ("z", "c")
    placed = (
        P(rows, None),
        P(),
        P(rows, None),
        P(rows, None),
        P(expert, "x", tensor),
        P(expert, "x", tensor),
        P(expert, tensor, "x"),
        P(rows, None, tensor, None),
        P(rows, tensor, None, None),
        P(rows, tensor),
    )
    return jax.shard_map(
        shards,
        mesh=fine,
        in_specs=placed,
        out_specs=(P(rows, tensor), P(rows, None, tensor, None)),
        check_vma=False,
    )
```

```python
import functools

import jax
import jax.numpy as jnp
from jax import lax
from jax.experimental import pallas as pl
from jax.experimental.pallas import tpu as pltpu
from jax.sharding import Mesh, PartitionSpec as P

LAT = 512
BF = jnp.bfloat16
F32 = jnp.float32
score_scale = 192.0 ** (-0.5)
VMEM = pl.BlockSpec(memory_space=pltpu.VMEM)
PARAMS = pltpu.CompilerParams(vmem_limit_bytes=48 * 1024 * 1024)
WIDE = pltpu.CompilerParams(vmem_limit_bytes=60 * 1024 * 1024)


def norm_kernel(tokens_ref, gain_ref, ids_ref, route_ref, down_ref, out_ref, mine_ref, send_ref):
    count = mine_ref.shape[1]
    side = lax.axis_index("h")
    for half in (0, 1):
        part = down_ref[:, half * count : (half + 1) * count]

        @pl.when(side == half)
        def _():
            mine_ref[...] = part

        @pl.when(side != half)
        def _():
            send_ref[...] = part

    values = tokens_ref[...].astype(F32)
    row_scale = lax.rsqrt(jnp.mean(values * values, axis=-1, keepdims=True) + 1e-06)
    normed = (values * row_scale * gain_ref[...]).astype(BF)
    parts, _, columns = out_ref.shape
    width = normed.shape[1] // parts
    experts = lax.axis_size("z") * lax.axis_size("c")
    ids, route = ids_ref[...], route_ref[...]
    table = jnp.concatenate(
        [
            jnp.sum(jnp.where(ids == expert, route, 0.0), axis=0, keepdims=True)
            for expert in range(experts)
        ],
        axis=0,
    )
    high = table.astype(BF)
    low = (table - high.astype(F32)).astype(BF)
    both = jnp.concatenate([high.astype(F32), low.astype(F32)], axis=0).astype(BF)
    shape = (2 * experts, columns - width)
    spread = lax.broadcasted_iota(jnp.int32, shape, 0) == lax.broadcasted_iota(jnp.int32, shape, 1)
    extra = lax.dot_general(
        both, spread.astype(F32).astype(BF), (((0,), (0,)), ((), ())), preferred_element_type=F32
    ).astype(BF)
    for part in range(parts):
        out_ref[part, :, :width] = normed[:, part * width : (part + 1) * width]
        out_ref[part, :, width:columns] = extra

def gate_up_kernel(rows_ref, gate_ref, up_ref, out_ref):
    z_count, cores, x_count, rows, width = rows_ref.shape
    me = lax.axis_index("c")
    flat = rows_ref[...].reshape(z_count * cores * x_count * rows, width)
    hidden = gate_ref.shape[1]
    for number, weight in enumerate((gate_ref, up_ref)):
        part = jnp.dot(flat, weight[...], preferred_element_type=F32).astype(BF)
        part = part.reshape(z_count, cores, x_count, rows, hidden)
        for core in range(cores):
            place = 1 - lax.rem(core + me, cores)
            for x in range(x_count):
                out_ref[x, place, :, :, number * hidden : (number + 1) * hidden] = part[:, core, x]


def active_kernel(parts_ref, out_ref):
    hidden = out_ref.shape[1]
    total = parts_ref[0].astype(F32)
    for x in range(1, parts_ref.shape[0]):
        total = total + parts_ref[x].astype(F32)
    gate, up = total[:, :hidden], total[:, hidden:]
    out_ref[...] = (gate / (1.0 + jnp.exp(-gate)) * up).astype(BF)


def down_kernel(place_ref, mine_ref, other_ref, route_ref, *refs):
    weights, added, out_ref = refs[:8], refs[8:-1], refs[-1]
    x_count = out_ref.shape[0]
    me = lax.axis_index("x")
    rows = mine_ref.shape[0]
    route = route_ref[...].reshape(rows, route_ref.shape[-1]).astype(F32)
    lane = lax.broadcasted_iota(jnp.int32, route.shape, 1)
    experts = lax.axis_size("z") * lax.axis_size("c")
    own = lax.axis_index("z") * lax.axis_size("c") + lax.axis_index("c")
    hit = (lane == own) | (lane == own + experts)
    coef = jnp.sum(jnp.where(hit, route, 0.0), axis=1, keepdims=True)
    for step, number in ((0, 0), (3, 2), (1, 4), (2, 6)):
        place = lax.rem(me + step, x_count)
        first = jnp.dot(mine_ref[...], weights[number][...], preferred_element_type=F32)
        second = jnp.dot(other_ref[...], weights[number + 1][...], preferred_element_type=F32)
        total = (first.astype(BF).astype(F32) + second.astype(BF).astype(F32)) * coef
        for ref in added:
            total = total + ref[place].astype(F32)
        out_ref[place] = total.astype(BF)


def attend_kernel(lengths_ref, queries_ref, cache_ref, out_ref):
    pieces, rows, heads, channels = queries_ref.shape
    latents = out_ref.shape[3]
    for row in range(rows):
        queries = queries_ref[:, row].reshape(pieces * heads, channels)
        cache = cache_ref[row]
        scores = jnp.dot(queries, cache, preferred_element_type=F32) * score_scale
        live = lax.broadcasted_iota(jnp.int32, scores.shape, 1) < lengths_ref[0, row]
        scores = jnp.where(live, scores, -1e30)
        exp_terms = jnp.exp(scores - jnp.max(scores, axis=1, keepdims=True))
        probs = (exp_terms / jnp.sum(exp_terms, axis=1, keepdims=True)).astype(BF)
        latent = lax.dot_general(
            probs, cache[:latents], (((1,), (1,)), ((), ())), preferred_element_type=F32
        )
        out_ref[:, row] = latent.astype(BF).reshape(pieces, heads, latents)


def attention(queries_b, cache_b, lengths_b):
    heads_dev, channels = queries_b.shape[2:]
    tensor_size = lax.axis_size("k") * lax.axis_size("h")
    rows_owned = cache_b.shape[1]
    asked = queries_b[0].reshape(tensor_size, rows_owned, heads_dev, channels)
    pieces = lax.all_to_all(asked, ("k", "h"), split_axis=0, concat_axis=0, tiled=True)
    return pl.pallas_call(
        attend_kernel,
        out_shape=jax.ShapeDtypeStruct((*pieces.shape[:3], LAT), BF),
        in_specs=[pl.BlockSpec(memory_space=pltpu.SMEM), VMEM, VMEM],
        out_specs=VMEM,
        compiler_params=WIDE,
        name="attend",
    )(lengths_b, pieces, cache_b[0].transpose(0, 2, 1))


def answer(result):
    answers = lax.all_to_all(result, ("k", "h"), split_axis=0, concat_axis=0, tiled=True)
    tensor_size, rows_owned, heads_dev, channels = answers.shape
    return answers.reshape(1, tensor_size * rows_owned, heads_dev, channels)


def swap(array, axis):
    return lax.ppermute(array, axis, [(0, 1), (1, 0)])


def shift(array, step):
    size = lax.axis_size("x")
    return lax.ppermute(array, "x", [(i, (i + step) % size) for i in range(size)])


def gate_up(gathered, w_gate, w_up):
    z_size, cores, x_size, rows, _ = gathered.shape
    width, hidden = w_gate.shape
    steps = 2
    partial = pl.pallas_call(
        gate_up_kernel,
        grid=(steps,),
        out_shape=jax.ShapeDtypeStruct((x_size, cores, z_size, rows, 2 * hidden), BF),
        in_specs=[
            pl.BlockSpec((z_size // steps, cores, x_size, rows, width), lambda i: (i, 0, 0, 0, 0)),
            pl.BlockSpec((width, hidden), lambda i: (0, 0)),
            pl.BlockSpec((width, hidden), lambda i: (0, 0)),
        ],
        out_specs=pl.BlockSpec(
            (x_size, cores, z_size // steps, rows, 2 * hidden), lambda i: (0, 0, i, 0, 0)
        ),
        compiler_params=WIDE,
        name="gate_up",
    )(gathered, w_gate, w_up)
    return partial.reshape(x_size, cores * z_size * rows, 2 * hidden)


def swiglu(parts):
    return pl.pallas_call(
        active_kernel,
        out_shape=jax.ShapeDtypeStruct((parts.shape[1], parts.shape[2] // 2), BF),
        in_specs=[VMEM],
        out_specs=VMEM,
        compiler_params=PARAMS,
        name="active_rows",
    )(parts)


def down(half, mine, other, gathered, place, weights, added):
    z_size, cores, x_size, rows, columns = gathered.shape
    count, hidden = mine.shape[0] // cores, mine.shape[1]
    lanes = 128
    last = columns // lanes - 1
    whole = pl.BlockSpec(memory_space=pltpu.VMEM)
    out_columns = weights[0].shape[1]
    return pl.pallas_call(
        down_kernel,
        out_shape=jax.ShapeDtypeStruct((x_size, count, out_columns), BF),
        grid_spec=pltpu.PrefetchScalarGridSpec(
            num_scalar_prefetch=1,
            grid=(1,),
            in_specs=[
                pl.BlockSpec((count, hidden), lambda i, p: (half, 0)),
                pl.BlockSpec((count, hidden), lambda i, p: (half, 0)),
                pl.BlockSpec((z_size, 1, 1, rows, lanes), lambda i, p: (0, p[0], p[1], 0, last)),
            ]
            + [whole] * (len(weights) + len(added)),
            out_specs=whole,
        ),
        compiler_params=PARAMS,
        name="down_rows",
    )(place, mine, other, gathered, *weights, *added)


def last_kernel(landed_ref, latent_ref, mixed_ref, latent_out_ref, sem):
    copy = pltpu.make_async_copy(latent_ref, latent_out_ref, sem)
    copy.start()
    total = landed_ref[0].astype(F32)
    for number in range(1, landed_ref.shape[0]):
        total = total + landed_ref[number].astype(F32)
    mixed_ref[...] = total.astype(BF)
    copy.wait()


def last(landed, latent):
    anywhere = pl.BlockSpec(memory_space=pl.ANY)
    return pl.pallas_call(
        last_kernel,
        out_shape=(
            jax.ShapeDtypeStruct(landed.shape[1:], BF),
            jax.ShapeDtypeStruct(latent.shape, BF),
        ),
        in_specs=[VMEM, anywhere],
        out_specs=(VMEM, anywhere),
        scratch_shapes=[pltpu.SemaphoreType.DMA],
        compiler_params=PARAMS,
        name="last_sum",
    )(landed, latent)


def shards(
    tokens_a,
    norm_gain,
    expert_ids,
    route_weights,
    w_gate,
    w_up,
    w_down,
    queries_b,
    cache_b,
    lengths_b,
):
    x_size, z_size, cores = lax.axis_size("x"), lax.axis_size("z"), lax.axis_size("c")
    rows = tokens_a.shape[0]
    width = w_gate.shape[1]
    lanes = 128

    columns = w_down.shape[2] // 2
    half_shape = jax.ShapeDtypeStruct((w_down.shape[1], columns), BF)
    normed, mine, send = pl.pallas_call(
        norm_kernel,
        grid=(1,),
        out_shape=(
            jax.ShapeDtypeStruct((x_size, rows, width + lanes), BF), half_shape, half_shape
        ),
        in_specs=[
            pl.BlockSpec(shape, lambda i: (0, 0))
            for shape in (tokens_a.shape, (1, norm_gain.shape[0])) + 2 * (expert_ids.shape[::-1],)
            + (w_down.shape[1:],)
        ],
        out_specs=(VMEM, VMEM, VMEM),
        compiler_params=WIDE,
        name="norm_rows",
    )(tokens_a, norm_gain.reshape(1, -1), expert_ids.T, route_weights.T, w_down[0])
    sliced = lax.all_to_all(normed, "x", split_axis=0, concat_axis=0, tiled=True)
    gathered = lax.all_gather(
        sliced.reshape(x_size * rows, width + lanes), ("z", "c"), axis=0, tiled=True
    ).reshape(z_size, cores, x_size, rows, width + lanes)

    theirs = swap(send, "h")
    mine_lower, mine_upper = shift(mine, 1), shift(mine, -1)
    theirs_lower, theirs_upper = shift(theirs, 1), shift(theirs, -1)
    across = (shift(mine_lower, 1), shift(theirs_upper, -1))
    weights = (mine, theirs, mine_lower, theirs_lower, mine_upper, theirs_upper, *across)

    result = attention(queries_b, cache_b, lengths_b)
    latent_b = answer(result)
    gathered, latent_b, near = lax.optimization_barrier((gathered, latent_b, weights[:6]))
    core, x_place = lax.axis_index("c"), lax.axis_index("x")
    partial = gate_up(gathered, w_gate[0], w_up[0])
    partial, across = lax.optimization_barrier((partial, across))
    weights = (*near, *across)
    parts = lax.all_to_all(partial, "x", split_axis=0, concat_axis=0, tiled=True)
    active = swiglu(parts)
    active_other = swap(active, "h")
    added = ()
    for half in range(cores):
        place = jnp.stack([lax.rem(core + 1 + half, cores), x_place])
        out = down(half, active, active_other, gathered, place, weights, added)
        if not added:
            added = (swap(out, "c"),)
    both = out.reshape(-1, rows, columns)
    landed = lax.all_to_all(both, ("k", "z"), split_axis=0, concat_axis=0, tiled=True)
    return last(landed, latent_b)


def solution(mesh):
    x_size, y_size, e_size = (mesh.shape[name] for name in ("dp", "tensor", "expert"))
    cores = 2
    fine = Mesh(
        mesh.devices.reshape(x_size, y_size // 2, 2, e_size // cores, cores),
        ("x", "k", "h", "z", "c"),
    )
    rows, tensor, expert = ("x", "z", "c"), ("k", "h"), ("z", "c")
    placed = (
        P(rows, None),
        P(),
        P(rows, None),
        P(rows, None),
        P(expert, "x", tensor),
        P(expert, "x", tensor),
        P(expert, tensor, "x"),
        P(rows, None, tensor, None),
        P(rows, tensor, None, None),
        P(rows, tensor),
    )
    return jax.shard_map(
        shards,
        mesh=fine,
        in_specs=placed,
        out_specs=(P(rows, tensor), P(rows, None, tensor, None)),
        check_vma=False,
    )
```

```python
import functools

import jax
import jax.numpy as jnp
from jax import lax
from jax.experimental import pallas as pl
from jax.experimental.pallas import tpu as pltpu
from jax.sharding import Mesh, PartitionSpec as P

LAT = 512
BF = jnp.bfloat16
F32 = jnp.float32
score_scale = 192.0 ** (-0.5)
VMEM = pl.BlockSpec(memory_space=pltpu.VMEM)
PARAMS = pltpu.CompilerParams(vmem_limit_bytes=48 * 1024 * 1024)
WIDE = pltpu.CompilerParams(vmem_limit_bytes=60 * 1024 * 1024)


def norm_kernel(tokens_ref, gain_ref, ids_ref, route_ref, down_ref, out_ref, mine_ref, send_ref):
    count = mine_ref.shape[1]
    side = lax.axis_index("h")
    for half in (0, 1):
        part = down_ref[:, half * count : (half + 1) * count]

        @pl.when(side == half)
        def _():
            mine_ref[...] = part

        @pl.when(side != half)
        def _():
            send_ref[...] = part

    values = tokens_ref[...].astype(F32)
    row_scale = lax.rsqrt(jnp.mean(values * values, axis=-1, keepdims=True) + 1e-06)
    normed = (values * row_scale * gain_ref[...]).astype(BF)
    parts, _, columns = out_ref.shape
    width = normed.shape[1] // parts
    experts = lax.axis_size("z") * lax.axis_size("c")
    ids, route = ids_ref[...], route_ref[...]
    table = jnp.concatenate(
        [
            jnp.sum(jnp.where(ids == expert, route, 0.0), axis=0, keepdims=True)
            for expert in range(experts)
        ],
        axis=0,
    )
    high = table.astype(BF)
    low = (table - high.astype(F32)).astype(BF)
    both = jnp.concatenate([high.astype(F32), low.astype(F32)], axis=0).astype(BF)
    shape = (2 * experts, columns - width)
    spread = lax.broadcasted_iota(jnp.int32, shape, 0) == lax.broadcasted_iota(jnp.int32, shape, 1)
    extra = lax.dot_general(
        both, spread.astype(F32).astype(BF), (((0,), (0,)), ((), ())), preferred_element_type=F32
    ).astype(BF)
    for part in range(parts):
        out_ref[part, :, :width] = normed[:, part * width : (part + 1) * width]
        out_ref[part, :, width:columns] = extra

def gate_up_kernel(rows_ref, gate_ref, up_ref, out_ref):
    z_count, cores, x_count, rows, width = rows_ref.shape
    me = lax.axis_index("c")
    flat = rows_ref[...].reshape(z_count * cores * x_count * rows, width)
    hidden = gate_ref.shape[1]
    for number, weight in enumerate((gate_ref, up_ref)):
        part = jnp.dot(flat, weight[...], preferred_element_type=F32).astype(BF)
        part = part.reshape(z_count, cores, x_count, rows, hidden)
        for core in range(cores):
            place = 1 - lax.rem(core + me, cores)
            for x in range(x_count):
                out_ref[x, place, :, :, number * hidden : (number + 1) * hidden] = part[:, core, x]


def active_kernel(parts_ref, out_ref):
    hidden = out_ref.shape[1]
    total = parts_ref[0].astype(F32)
    for x in range(1, parts_ref.shape[0]):
        total = total + parts_ref[x].astype(F32)
    gate, up = total[:, :hidden], total[:, hidden:]
    out_ref[...] = (gate / (1.0 + jnp.exp(-gate)) * up).astype(BF)


def down_kernel(place_ref, mine_ref, other_ref, route_ref, own_route_ref, *refs):
    weights, (send_ref, keep_ref) = refs[:8], refs[8:]
    x_count, half = send_ref.shape[:2]
    me = lax.axis_index("x")
    rows = mine_ref.shape[0]
    route = jnp.concatenate(
        [ref[...].reshape(half, ref.shape[-1]).astype(F32) for ref in (route_ref, own_route_ref)],
        axis=0,
    )
    lane = lax.broadcasted_iota(jnp.int32, route.shape, 1)
    experts = lax.axis_size("z") * lax.axis_size("c")
    own = lax.axis_index("z") * lax.axis_size("c") + lax.axis_index("c")
    hit = (lane == own) | (lane == own + experts)
    coef = jnp.sum(jnp.where(hit, route, 0.0), axis=1, keepdims=True)
    for step, number in ((0, 0), (3, 2), (1, 4), (2, 6)):
        place = lax.rem(me + step, x_count)
        first = jnp.dot(mine_ref[...], weights[number][...], preferred_element_type=F32)
        second = jnp.dot(other_ref[...], weights[number + 1][...], preferred_element_type=F32)
        total = (first.astype(BF).astype(F32) + second.astype(BF).astype(F32)) * coef
        send_ref[place] = total[:half].astype(BF)
        keep_ref[place] = total[half:]


def attend_kernel(lengths_ref, queries_ref, cache_ref, out_ref):
    pieces, rows, heads, channels = queries_ref.shape
    latents = out_ref.shape[3]
    for row in range(rows):
        queries = queries_ref[:, row].reshape(pieces * heads, channels)
        cache = cache_ref[row]
        scores = jnp.dot(queries, cache, preferred_element_type=F32) * score_scale
        live = lax.broadcasted_iota(jnp.int32, scores.shape, 1) < lengths_ref[0, row]
        scores = jnp.where(live, scores, -1e30)
        exp_terms = jnp.exp(scores - jnp.max(scores, axis=1, keepdims=True))
        probs = (exp_terms / jnp.sum(exp_terms, axis=1, keepdims=True)).astype(BF)
        latent = lax.dot_general(
            probs, cache[:latents], (((1,), (1,)), ((), ())), preferred_element_type=F32
        )
        out_ref[:, row] = latent.astype(BF).reshape(pieces, heads, latents)


def attention(queries_b, cache_b, lengths_b, beside):
    heads_dev, channels = queries_b.shape[2:]
    tensor_size = lax.axis_size("k") * lax.axis_size("h")
    rows_owned = cache_b.shape[1]
    asked = queries_b[0].reshape(tensor_size, rows_owned, heads_dev, channels)
    pieces = lax.all_to_all(asked, ("k", "h"), split_axis=0, concat_axis=0, tiled=True)
    pieces, beside = lax.optimization_barrier((pieces, beside))
    result = pl.pallas_call(
        attend_kernel,
        out_shape=jax.ShapeDtypeStruct((*pieces.shape[:3], LAT), BF),
        in_specs=[pl.BlockSpec(memory_space=pltpu.SMEM), VMEM, VMEM],
        out_specs=VMEM,
        compiler_params=WIDE,
        name="attend",
    )(lengths_b, pieces, cache_b[0].transpose(0, 2, 1))
    return result, beside


def answer(result):
    answers = lax.all_to_all(result, ("k", "h"), split_axis=0, concat_axis=0, tiled=True)
    tensor_size, rows_owned, heads_dev, channels = answers.shape
    return answers.reshape(1, tensor_size * rows_owned, heads_dev, channels)


def swap(array, axis):
    return lax.ppermute(array, axis, [(0, 1), (1, 0)])


def shift(array, step):
    size = lax.axis_size("x")
    return lax.ppermute(array, "x", [(i, (i + step) % size) for i in range(size)])


def gate_up(gathered, w_gate, w_up):
    z_size, cores, x_size, rows, _ = gathered.shape
    width, hidden = w_gate.shape
    steps = 2
    partial = pl.pallas_call(
        gate_up_kernel,
        grid=(steps,),
        out_shape=jax.ShapeDtypeStruct((x_size, cores, z_size, rows, 2 * hidden), BF),
        in_specs=[
            pl.BlockSpec((z_size // steps, cores, x_size, rows, width), lambda i: (i, 0, 0, 0, 0)),
            pl.BlockSpec((width, hidden), lambda i: (0, 0)),
            pl.BlockSpec((width, hidden), lambda i: (0, 0)),
        ],
        out_specs=pl.BlockSpec(
            (x_size, cores, z_size // steps, rows, 2 * hidden), lambda i: (0, 0, i, 0, 0)
        ),
        compiler_params=WIDE,
        name="gate_up",
    )(gathered, w_gate, w_up)
    return partial.reshape(x_size, cores * z_size * rows, 2 * hidden)


def swiglu(parts):
    return pl.pallas_call(
        active_kernel,
        out_shape=jax.ShapeDtypeStruct((parts.shape[1], parts.shape[2] // 2), BF),
        in_specs=[VMEM],
        out_specs=VMEM,
        compiler_params=PARAMS,
        name="active_rows",
    )(parts)


def down(mine, other, gathered, place, weights):
    z_size, cores, x_size, rows, columns = gathered.shape
    count, hidden = mine.shape
    lanes = 128
    last_lanes = columns // lanes - 1
    whole = pl.BlockSpec(memory_space=pltpu.VMEM)
    shape = (x_size, count // cores, weights[0].shape[1])
    return pl.pallas_call(
        down_kernel,
        out_shape=(jax.ShapeDtypeStruct(shape, BF), jax.ShapeDtypeStruct(shape, F32)),
        grid_spec=pltpu.PrefetchScalarGridSpec(
            num_scalar_prefetch=1,
            grid=(1,),
            in_specs=[
                whole,
                whole,
                pl.BlockSpec((z_size, 1, 1, rows, lanes), lambda i, p: (0, p[0], p[1], 0, last_lanes)),
                pl.BlockSpec((z_size, 1, 1, rows, lanes), lambda i, p: (0, 1 - p[0], p[1], 0, last_lanes)),
            ]
            + [whole] * len(weights),
            out_specs=(whole, whole),
        ),
        compiler_params=PARAMS,
        name="down_rows",
    )(place, mine, other, gathered, gathered, *weights)


def last_kernel(landed_ref, latent_ref, mixed_ref, latent_out_ref, sem):
    copy = pltpu.make_async_copy(latent_ref, latent_out_ref, sem)
    copy.start()
    total = landed_ref[0].astype(F32)
    for number in range(1, landed_ref.shape[0]):
        total = total + landed_ref[number].astype(F32)
    mixed_ref[...] = total.astype(BF)
    copy.wait()


def last(landed, latent):
    anywhere = pl.BlockSpec(memory_space=pl.ANY)
    return pl.pallas_call(
        last_kernel,
        out_shape=(
            jax.ShapeDtypeStruct(landed.shape[1:], BF),
            jax.ShapeDtypeStruct(latent.shape, BF),
        ),
        in_specs=[VMEM, anywhere],
        out_specs=(VMEM, anywhere),
        scratch_shapes=[pltpu.SemaphoreType.DMA],
        compiler_params=PARAMS,
        name="last_sum",
    )(landed, latent)


def shards(
    tokens_a,
    norm_gain,
    expert_ids,
    route_weights,
    w_gate,
    w_up,
    w_down,
    queries_b,
    cache_b,
    lengths_b,
):
    x_size, z_size, cores = lax.axis_size("x"), lax.axis_size("z"), lax.axis_size("c")
    rows = tokens_a.shape[0]
    width = w_gate.shape[1]
    lanes = 128

    columns = w_down.shape[2] // 2
    half_shape = jax.ShapeDtypeStruct((w_down.shape[1], columns), BF)
    normed, mine, send = pl.pallas_call(
        norm_kernel,
        grid=(1,),
        out_shape=(
            jax.ShapeDtypeStruct((x_size, rows, width + lanes), BF), half_shape, half_shape
        ),
        in_specs=[
            pl.BlockSpec(shape, lambda i: (0, 0))
            for shape in (tokens_a.shape, (1, norm_gain.shape[0])) + 2 * (expert_ids.shape[::-1],)
            + (w_down.shape[1:],)
        ],
        out_specs=(VMEM, VMEM, VMEM),
        compiler_params=WIDE,
        name="norm_rows",
    )(tokens_a, norm_gain.reshape(1, -1), expert_ids.T, route_weights.T, w_down[0])
    sliced = lax.all_to_all(normed, "x", split_axis=0, concat_axis=0, tiled=True)
    gathered = lax.all_gather(
        sliced.reshape(x_size * rows, width + lanes), ("z", "c"), axis=0, tiled=True
    ).reshape(z_size, cores, x_size, rows, width + lanes)

    theirs = swap(send, "h")
    mine_lower, mine_upper = shift(mine, 1), shift(mine, -1)
    theirs_lower, theirs_upper = shift(theirs, 1), shift(theirs, -1)
    across = (shift(mine_lower, 1), shift(theirs_upper, -1))
    result, mine_upper = attention(queries_b, cache_b, lengths_b, mine_upper)
    weights = (mine, theirs, mine_lower, theirs_lower, mine_upper, theirs_upper, *across)

    latent_b = answer(result)
    gathered, latent_b, near = lax.optimization_barrier((gathered, latent_b, weights[:6]))
    core, x_place = lax.axis_index("c"), lax.axis_index("x")
    partial = gate_up(gathered, w_gate[0], w_up[0])
    partial, across = lax.optimization_barrier((partial, across))
    weights = (*near, *across)
    parts = lax.all_to_all(partial, "x", split_axis=0, concat_axis=0, tiled=True)
    active = swiglu(parts)
    active_other = swap(active, "h")
    place = jnp.stack([lax.rem(core + 1, cores), x_place])
    sent, kept = down(active, active_other, gathered, place, weights)
    out = (kept + swap(sent, "c").astype(F32)).astype(BF)
    both = out.reshape(-1, rows, columns)
    landed = lax.all_to_all(both, ("k", "z"), split_axis=0, concat_axis=0, tiled=True)
    return last(landed, latent_b)


def solution(mesh):
    x_size, y_size, e_size = (mesh.shape[name] for name in ("dp", "tensor", "expert"))
    cores = 2
    fine = Mesh(
        mesh.devices.reshape(x_size, y_size // 2, 2, e_size // cores, cores),
        ("x", "k", "h", "z", "c"),
    )
    rows, tensor, expert = ("x", "z", "c"), ("k", "h"), ("z", "c")
    placed = (
        P(rows, None),
        P(),
        P(rows, None),
        P(rows, None),
        P(expert, "x", tensor),
        P(expert, "x", tensor),
        P(expert, tensor, "x"),
        P(rows, None, tensor, None),
        P(rows, tensor, None, None),
        P(rows, tensor),
    )
    return jax.shard_map(
        shards,
        mesh=fine,
        in_specs=placed,
        out_specs=(P(rows, tensor), P(rows, None, tensor, None)),
        check_vma=False,
    )
```

```python
import functools

import jax
import jax.numpy as jnp
from jax import lax
from jax.experimental import pallas as pl
from jax.experimental.pallas import tpu as pltpu
from jax.sharding import Mesh, PartitionSpec as P

LAT = 512
BF = jnp.bfloat16
F32 = jnp.float32
score_scale = 192.0 ** (-0.5)
VMEM = pl.BlockSpec(memory_space=pltpu.VMEM)
PARAMS = pltpu.CompilerParams(vmem_limit_bytes=48 * 1024 * 1024)
WIDE = pltpu.CompilerParams(vmem_limit_bytes=60 * 1024 * 1024)


def norm_kernel(tokens_ref, gain_ref, ids_ref, route_ref, down_ref, out_ref, mine_ref, send_ref):
    count = mine_ref.shape[1]
    side = lax.axis_index("h")
    for half in (0, 1):
        part = down_ref[:, half * count : (half + 1) * count]

        @pl.when(side == half)
        def _():
            mine_ref[...] = part

        @pl.when(side != half)
        def _():
            send_ref[...] = part

    values = tokens_ref[...].astype(F32)
    row_scale = lax.rsqrt(jnp.mean(values * values, axis=-1, keepdims=True) + 1e-06)
    normed = (values * row_scale * gain_ref[...]).astype(BF)
    parts, _, columns = out_ref.shape
    width = normed.shape[1] // parts
    experts = lax.axis_size("z") * lax.axis_size("c")
    ids, route = ids_ref[...], route_ref[...]
    table = jnp.concatenate(
        [
            jnp.sum(jnp.where(ids == expert, route, 0.0), axis=0, keepdims=True)
            for expert in range(experts)
        ],
        axis=0,
    )
    high = table.astype(BF)
    low = (table - high.astype(F32)).astype(BF)
    both = jnp.concatenate([high.astype(F32), low.astype(F32)], axis=0).astype(BF)
    shape = (2 * experts, columns - width)
    spread = lax.broadcasted_iota(jnp.int32, shape, 0) == lax.broadcasted_iota(jnp.int32, shape, 1)
    extra = lax.dot_general(
        both, spread.astype(F32).astype(BF), (((0,), (0,)), ((), ())), preferred_element_type=F32
    ).astype(BF)
    for part in range(parts):
        out_ref[part, :, :width] = normed[:, part * width : (part + 1) * width]
        out_ref[part, :, width:columns] = extra

def gate_up_kernel(rows_ref, gate_ref, up_ref, out_ref):
    z_count, cores, x_count, rows, width = rows_ref.shape
    me = lax.axis_index("c")
    flat = rows_ref[...].reshape(z_count * cores * x_count * rows, width)
    hidden = gate_ref.shape[1]
    for number, weight in enumerate((gate_ref, up_ref)):
        part = jnp.dot(flat, weight[...], preferred_element_type=F32).astype(BF)
        part = part.reshape(z_count, cores, x_count, rows, hidden)
        for core in range(cores):
            place = 1 - lax.rem(core + me, cores)
            for x in range(x_count):
                out_ref[x, place, :, :, number * hidden : (number + 1) * hidden] = part[:, core, x]


def active_kernel(parts_ref, out_ref):
    hidden = out_ref.shape[1]
    total = parts_ref[0].astype(F32)
    for x in range(1, parts_ref.shape[0]):
        total = total + parts_ref[x].astype(F32)
    gate, up = total[:, :hidden], total[:, hidden:]
    out_ref[...] = (gate / (1.0 + jnp.exp(-gate)) * up).astype(BF)


def down_kernel(place_ref, mine_ref, other_ref, route_ref, own_route_ref, *refs):
    weights, (send_ref, keep_ref) = refs[:8], refs[8:]
    x_count, half = send_ref.shape[:2]
    me = lax.axis_index("x")
    rows = mine_ref.shape[0]
    route = jnp.concatenate(
        [ref[...].reshape(half, ref.shape[-1]).astype(F32) for ref in (route_ref, own_route_ref)],
        axis=0,
    )
    lane = lax.broadcasted_iota(jnp.int32, route.shape, 1)
    experts = lax.axis_size("z") * lax.axis_size("c")
    own = lax.axis_index("z") * lax.axis_size("c") + lax.axis_index("c")
    hit = (lane == own) | (lane == own + experts)
    coef = jnp.sum(jnp.where(hit, route, 0.0), axis=1, keepdims=True)
    for step, number in ((0, 0), (3, 2), (1, 4), (2, 6)):
        place = lax.rem(me + step, x_count)
        first = jnp.dot(mine_ref[...], weights[number][...], preferred_element_type=F32)
        second = jnp.dot(other_ref[...], weights[number + 1][...], preferred_element_type=F32)
        total = (first.astype(BF).astype(F32) + second.astype(BF).astype(F32)) * coef
        send_ref[place] = total[:half].astype(BF)
        keep_ref[place] = total[half:].astype(BF)


def attend_kernel(lengths_ref, queries_ref, cache_ref, out_ref):
    pieces, rows, heads, channels = queries_ref.shape
    latents = out_ref.shape[3]
    for row in range(rows):
        queries = queries_ref[:, row].reshape(pieces * heads, channels)
        cache = cache_ref[row]
        scores = jnp.dot(queries, cache, preferred_element_type=F32) * score_scale
        live = lax.broadcasted_iota(jnp.int32, scores.shape, 1) < lengths_ref[0, row]
        scores = jnp.where(live, scores, -1e30)
        exp_terms = jnp.exp(scores - jnp.max(scores, axis=1, keepdims=True))
        probs = (exp_terms / jnp.sum(exp_terms, axis=1, keepdims=True)).astype(BF)
        latent = lax.dot_general(
            probs, cache[:latents], (((1,), (1,)), ((), ())), preferred_element_type=F32
        )
        out_ref[:, row] = latent.astype(BF).reshape(pieces, heads, latents)


def attention(queries_b, cache_b, lengths_b, beside):
    heads_dev, channels = queries_b.shape[2:]
    tensor_size = lax.axis_size("k") * lax.axis_size("h")
    rows_owned = cache_b.shape[1]
    asked = queries_b[0].reshape(tensor_size, rows_owned, heads_dev, channels)
    pieces = lax.all_to_all(asked, ("k", "h"), split_axis=0, concat_axis=0, tiled=True)
    pieces, beside = lax.optimization_barrier((pieces, beside))
    result = pl.pallas_call(
        attend_kernel,
        out_shape=jax.ShapeDtypeStruct((*pieces.shape[:3], LAT), BF),
        in_specs=[pl.BlockSpec(memory_space=pltpu.SMEM), VMEM, VMEM],
        out_specs=VMEM,
        compiler_params=WIDE,
        name="attend",
    )(lengths_b, pieces, cache_b[0].transpose(0, 2, 1))
    return result, beside


def answer(result):
    answers = lax.all_to_all(result, ("k", "h"), split_axis=0, concat_axis=0, tiled=True)
    tensor_size, rows_owned, heads_dev, channels = answers.shape
    return answers.reshape(1, tensor_size * rows_owned, heads_dev, channels)


def swap(array, axis):
    return lax.ppermute(array, axis, [(0, 1), (1, 0)])


def shift(array, step):
    size = lax.axis_size("x")
    return lax.ppermute(array, "x", [(i, (i + step) % size) for i in range(size)])


def gate_up(gathered, w_gate, w_up):
    z_size, cores, x_size, rows, _ = gathered.shape
    width, hidden = w_gate.shape
    steps = 2
    partial = pl.pallas_call(
        gate_up_kernel,
        grid=(steps,),
        out_shape=jax.ShapeDtypeStruct((x_size, cores, z_size, rows, 2 * hidden), BF),
        in_specs=[
            pl.BlockSpec((z_size // steps, cores, x_size, rows, width), lambda i: (i, 0, 0, 0, 0)),
            pl.BlockSpec((width, hidden), lambda i: (0, 0)),
            pl.BlockSpec((width, hidden), lambda i: (0, 0)),
        ],
        out_specs=pl.BlockSpec(
            (x_size, cores, z_size // steps, rows, 2 * hidden), lambda i: (0, 0, i, 0, 0)
        ),
        compiler_params=WIDE,
        name="gate_up",
    )(gathered, w_gate, w_up)
    return partial.reshape(x_size, cores * z_size * rows, 2 * hidden)


def swiglu(parts):
    return pl.pallas_call(
        active_kernel,
        out_shape=jax.ShapeDtypeStruct((parts.shape[1], parts.shape[2] // 2), BF),
        in_specs=[VMEM],
        out_specs=VMEM,
        compiler_params=PARAMS,
        name="active_rows",
    )(parts)


def down(mine, other, gathered, place, weights):
    z_size, cores, x_size, rows, columns = gathered.shape
    count, hidden = mine.shape
    lanes = 128
    last_lanes = columns // lanes - 1
    whole = pl.BlockSpec(memory_space=pltpu.VMEM)
    shape = (x_size, count // cores, weights[0].shape[1])
    return pl.pallas_call(
        down_kernel,
        out_shape=(jax.ShapeDtypeStruct(shape, BF), jax.ShapeDtypeStruct(shape, BF)),
        grid_spec=pltpu.PrefetchScalarGridSpec(
            num_scalar_prefetch=1,
            grid=(1,),
            in_specs=[
                whole,
                whole,
                pl.BlockSpec((z_size, 1, 1, rows, lanes), lambda i, p: (0, p[0], p[1], 0, last_lanes)),
                pl.BlockSpec((z_size, 1, 1, rows, lanes), lambda i, p: (0, 1 - p[0], p[1], 0, last_lanes)),
            ]
            + [whole] * len(weights),
            out_specs=(whole, whole),
        ),
        compiler_params=PARAMS,
        name="down_rows",
    )(place, mine, other, gathered, gathered, *weights)


def last_kernel(landed_ref, latent_ref, mixed_ref, latent_out_ref, sem):
    copy = pltpu.make_async_copy(latent_ref, latent_out_ref, sem)
    copy.start()
    total = landed_ref[0].astype(F32)
    for number in range(1, landed_ref.shape[0]):
        total = total + landed_ref[number].astype(F32)
    mixed_ref[...] = total.astype(BF)
    copy.wait()


def last(landed, latent):
    anywhere = pl.BlockSpec(memory_space=pl.ANY)
    return pl.pallas_call(
        last_kernel,
        out_shape=(
            jax.ShapeDtypeStruct(landed.shape[1:], BF),
            jax.ShapeDtypeStruct(latent.shape, BF),
        ),
        in_specs=[VMEM, anywhere],
        out_specs=(VMEM, anywhere),
        scratch_shapes=[pltpu.SemaphoreType.DMA],
        compiler_params=PARAMS,
        name="last_sum",
    )(landed, latent)


def shards(
    tokens_a,
    norm_gain,
    expert_ids,
    route_weights,
    w_gate,
    w_up,
    w_down,
    queries_b,
    cache_b,
    lengths_b,
):
    x_size, z_size, cores = lax.axis_size("x"), lax.axis_size("z"), lax.axis_size("c")
    rows = tokens_a.shape[0]
    width = w_gate.shape[1]
    lanes = 128

    columns = w_down.shape[2] // 2
    half_shape = jax.ShapeDtypeStruct((w_down.shape[1], columns), BF)
    normed, mine, send = pl.pallas_call(
        norm_kernel,
        grid=(1,),
        out_shape=(
            jax.ShapeDtypeStruct((x_size, rows, width + lanes), BF), half_shape, half_shape
        ),
        in_specs=[
            pl.BlockSpec(shape, lambda i: (0, 0))
            for shape in (tokens_a.shape, (1, norm_gain.shape[0])) + 2 * (expert_ids.shape[::-1],)
            + (w_down.shape[1:],)
        ],
        out_specs=(VMEM, VMEM, VMEM),
        compiler_params=WIDE,
        name="norm_rows",
    )(tokens_a, norm_gain.reshape(1, -1), expert_ids.T, route_weights.T, w_down[0])
    sliced = lax.all_to_all(normed, "x", split_axis=0, concat_axis=0, tiled=True)
    gathered = lax.all_gather(
        sliced.reshape(x_size * rows, width + lanes), ("z", "c"), axis=0, tiled=True
    ).reshape(z_size, cores, x_size, rows, width + lanes)

    theirs = swap(send, "h")
    mine_lower, mine_upper = shift(mine, 1), shift(mine, -1)
    theirs_lower, theirs_upper = shift(theirs, 1), shift(theirs, -1)
    across = (shift(mine_lower, 1), shift(theirs_upper, -1))
    result, mine_upper = attention(queries_b, cache_b, lengths_b, mine_upper)
    weights = (mine, theirs, mine_lower, theirs_lower, mine_upper, theirs_upper, *across)

    latent_b = answer(result)
    gathered, latent_b, near = lax.optimization_barrier((gathered, latent_b, weights[:6]))
    core, x_place = lax.axis_index("c"), lax.axis_index("x")
    partial = gate_up(gathered, w_gate[0], w_up[0])
    partial, across = lax.optimization_barrier((partial, across))
    weights = (*near, *across)
    parts = lax.all_to_all(partial, "x", split_axis=0, concat_axis=0, tiled=True)
    active = swiglu(parts)
    active_other = swap(active, "h")
    place = jnp.stack([lax.rem(core + 1, cores), x_place])
    sent, kept = down(active, active_other, gathered, place, weights)
    out = (kept.astype(F32) + swap(sent, "c").astype(F32)).astype(BF)
    both = out.reshape(-1, rows, columns)
    landed = lax.all_to_all(both, ("k", "z"), split_axis=0, concat_axis=0, tiled=True)
    return last(landed, latent_b)


def solution(mesh):
    x_size, y_size, e_size = (mesh.shape[name] for name in ("dp", "tensor", "expert"))
    cores = 2
    fine = Mesh(
        mesh.devices.reshape(x_size, y_size // 2, 2, e_size // cores, cores),
        ("x", "k", "h", "z", "c"),
    )
    rows, tensor, expert = ("x", "z", "c"), ("k", "h"), ("z", "c")
    placed = (
        P(rows, None),
        P(),
        P(rows, None),
        P(rows, None),
        P(expert, "x", tensor),
        P(expert, "x", tensor),
        P(expert, tensor, "x"),
        P(rows, None, tensor, None),
        P(rows, tensor, None, None),
        P(rows, tensor),
    )
    return jax.shard_map(
        shards,
        mesh=fine,
        in_specs=placed,
        out_specs=(P(rows, tensor), P(rows, None, tensor, None)),
        check_vma=False,
    )
```

```python
import functools

import jax
import jax.numpy as jnp
from jax import lax
from jax.experimental import pallas as pl
from jax.experimental.pallas import tpu as pltpu
from jax.sharding import Mesh, PartitionSpec as P

LAT = 512
BF = jnp.bfloat16
F32 = jnp.float32
score_scale = 192.0 ** (-0.5)
VMEM = pl.BlockSpec(memory_space=pltpu.VMEM)
PARAMS = pltpu.CompilerParams(vmem_limit_bytes=48 * 1024 * 1024)
WIDE = pltpu.CompilerParams(vmem_limit_bytes=57 * 1024 * 1024)


def norm_kernel(tokens_ref, gain_ref, ids_ref, route_ref, down_ref, out_ref, mine_ref, send_ref):
    count = mine_ref.shape[1]
    side = lax.axis_index("h")
    for half in (0, 1):
        part = down_ref[:, half * count : (half + 1) * count]

        @pl.when(side == half)
        def _():
            mine_ref[...] = part

        @pl.when(side != half)
        def _():
            send_ref[...] = part

    values = tokens_ref[...].astype(F32)
    row_scale = lax.rsqrt(jnp.mean(values * values, axis=-1, keepdims=True) + 1e-06)
    normed = (values * row_scale * gain_ref[...]).astype(BF)
    parts, _, columns = out_ref.shape
    width = normed.shape[1] // parts
    experts = lax.axis_size("z") * lax.axis_size("c")
    ids, route = ids_ref[...], route_ref[...]
    table = jnp.concatenate(
        [
            jnp.sum(jnp.where(ids == expert, route, 0.0), axis=0, keepdims=True)
            for expert in range(experts)
        ],
        axis=0,
    )
    high = table.astype(BF)
    low = (table - high.astype(F32)).astype(BF)
    both = jnp.concatenate([high.astype(F32), low.astype(F32)], axis=0).astype(BF)
    shape = (2 * experts, columns - width)
    spread = lax.broadcasted_iota(jnp.int32, shape, 0) == lax.broadcasted_iota(jnp.int32, shape, 1)
    extra = lax.dot_general(
        both, spread.astype(F32).astype(BF), (((0,), (0,)), ((), ())), preferred_element_type=F32
    ).astype(BF)
    for part in range(parts):
        out_ref[part, :, :width] = normed[:, part * width : (part + 1) * width]
        out_ref[part, :, width:columns] = extra

def gate_up_kernel(rows_ref, gate_ref, up_ref, out_ref):
    z_count, cores, x_count, rows, width = rows_ref.shape
    me = lax.axis_index("c")
    flat = rows_ref[...].reshape(z_count * cores * x_count * rows, width)
    hidden = gate_ref.shape[1]
    for number, weight in enumerate((gate_ref, up_ref)):
        part = jnp.dot(flat, weight[...], preferred_element_type=F32).astype(BF)
        part = part.reshape(z_count, cores, x_count, rows, hidden)
        for core in range(cores):
            place = 1 - lax.rem(core + me, cores)
            for x in range(x_count):
                out_ref[x, place, :, :, number * hidden : (number + 1) * hidden] = part[:, core, x]


def active_kernel(parts_ref, out_ref):
    hidden = out_ref.shape[1]
    total = parts_ref[0].astype(F32)
    for x in range(1, parts_ref.shape[0]):
        total = total + parts_ref[x].astype(F32)
    gate, up = total[:, :hidden], total[:, hidden:]
    out_ref[...] = (gate / (1.0 + jnp.exp(-gate)) * up).astype(BF)


def down_kernel(place_ref, mine_ref, other_ref, route_ref, own_route_ref, *refs):
    weights, (send_ref, keep_ref) = refs[:8], refs[8:]
    x_count, half = send_ref.shape[:2]
    me = lax.axis_index("x")
    rows = mine_ref.shape[0]
    route = jnp.concatenate(
        [ref[...].reshape(half, ref.shape[-1]).astype(F32) for ref in (route_ref, own_route_ref)],
        axis=0,
    )
    lane = lax.broadcasted_iota(jnp.int32, route.shape, 1)
    experts = lax.axis_size("z") * lax.axis_size("c")
    own = lax.axis_index("z") * lax.axis_size("c") + lax.axis_index("c")
    hit = (lane == own) | (lane == own + experts)
    coef = jnp.sum(jnp.where(hit, route, 0.0), axis=1, keepdims=True)
    for step, number in ((0, 0), (3, 2), (1, 4), (2, 6)):
        place = lax.rem(me + step, x_count)
        first = jnp.dot(mine_ref[...], weights[number][...], preferred_element_type=F32)
        second = jnp.dot(other_ref[...], weights[number + 1][...], preferred_element_type=F32)
        total = (first.astype(BF).astype(F32) + second.astype(BF).astype(F32)) * coef
        send_ref[place] = total[:half].astype(BF)
        keep_ref[place] = total[half:].astype(BF)


def attend_kernel(lengths_ref, queries_ref, cache_ref, out_ref):
    pieces, rows, heads, channels = queries_ref.shape
    latents = out_ref.shape[3]
    for row in range(rows):
        queries = queries_ref[:, row].reshape(pieces * heads, channels)
        cache = cache_ref[row]
        scores = jnp.dot(queries, cache, preferred_element_type=F32) * score_scale
        live = lax.broadcasted_iota(jnp.int32, scores.shape, 1) < lengths_ref[0, row]
        scores = jnp.where(live, scores, -1e30)
        exp_terms = jnp.exp(scores - jnp.max(scores, axis=1, keepdims=True))
        probs = (exp_terms / jnp.sum(exp_terms, axis=1, keepdims=True)).astype(BF)
        latent = lax.dot_general(
            probs, cache[:latents], (((1,), (1,)), ((), ())), preferred_element_type=F32
        )
        out_ref[:, row] = latent.astype(BF).reshape(pieces, heads, latents)


def attention(queries_b, cache_b, lengths_b, beside):
    heads_dev, channels = queries_b.shape[2:]
    tensor_size = lax.axis_size("k") * lax.axis_size("h")
    rows_owned = cache_b.shape[1]
    asked = queries_b[0].reshape(tensor_size, rows_owned, heads_dev, channels)
    pieces = lax.all_to_all(asked, ("k", "h"), split_axis=0, concat_axis=0, tiled=True)
    pieces, beside = lax.optimization_barrier((pieces, beside))
    result = pl.pallas_call(
        attend_kernel,
        out_shape=jax.ShapeDtypeStruct((*pieces.shape[:3], LAT), BF),
        in_specs=[pl.BlockSpec(memory_space=pltpu.SMEM), VMEM, VMEM],
        out_specs=VMEM,
        compiler_params=WIDE,
        name="attend",
    )(lengths_b, pieces, cache_b[0].transpose(0, 2, 1))
    return result, beside


def answer(result):
    answers = lax.all_to_all(result, ("k", "h"), split_axis=0, concat_axis=0, tiled=True)
    tensor_size, rows_owned, heads_dev, channels = answers.shape
    return answers.reshape(1, tensor_size * rows_owned, heads_dev, channels)


def swap(array, axis):
    return lax.ppermute(array, axis, [(0, 1), (1, 0)])


def shift(array, step):
    size = lax.axis_size("x")
    return lax.ppermute(array, "x", [(i, (i + step) % size) for i in range(size)])


def gate_up(gathered, w_gate, w_up):
    z_size, cores, x_size, rows, _ = gathered.shape
    width, hidden = w_gate.shape
    steps = 2
    partial = pl.pallas_call(
        gate_up_kernel,
        grid=(steps,),
        out_shape=jax.ShapeDtypeStruct((x_size, cores, z_size, rows, 2 * hidden), BF),
        in_specs=[
            pl.BlockSpec((z_size // steps, cores, x_size, rows, width), lambda i: (i, 0, 0, 0, 0)),
            pl.BlockSpec((width, hidden), lambda i: (0, 0)),
            pl.BlockSpec((width, hidden), lambda i: (0, 0)),
        ],
        out_specs=pl.BlockSpec(
            (x_size, cores, z_size // steps, rows, 2 * hidden), lambda i: (0, 0, i, 0, 0)
        ),
        compiler_params=WIDE,
        name="gate_up",
    )(gathered, w_gate, w_up)
    return partial.reshape(x_size, cores * z_size * rows, 2 * hidden)


def swiglu(parts):
    return pl.pallas_call(
        active_kernel,
        out_shape=jax.ShapeDtypeStruct((parts.shape[1], parts.shape[2] // 2), BF),
        in_specs=[VMEM],
        out_specs=VMEM,
        compiler_params=PARAMS,
        name="active_rows",
    )(parts)


def down(mine, other, gathered, place, weights):
    z_size, cores, x_size, rows, columns = gathered.shape
    count, hidden = mine.shape
    lanes = 128
    last_lanes = columns // lanes - 1
    whole = pl.BlockSpec(memory_space=pltpu.VMEM)
    shape = (x_size, count // cores, weights[0].shape[1])
    return pl.pallas_call(
        down_kernel,
        out_shape=(jax.ShapeDtypeStruct(shape, BF), jax.ShapeDtypeStruct(shape, BF)),
        grid_spec=pltpu.PrefetchScalarGridSpec(
            num_scalar_prefetch=1,
            grid=(1,),
            in_specs=[
                whole,
                whole,
                pl.BlockSpec((z_size, 1, 1, rows, lanes), lambda i, p: (0, p[0], p[1], 0, last_lanes)),
                pl.BlockSpec((z_size, 1, 1, rows, lanes), lambda i, p: (0, 1 - p[0], p[1], 0, last_lanes)),
            ]
            + [whole] * len(weights),
            out_specs=(whole, whole),
        ),
        compiler_params=PARAMS,
        name="down_rows",
    )(place, mine, other, gathered, gathered, *weights)


def last_kernel(landed_ref, latent_ref, mixed_ref, latent_out_ref, sem):
    copy = pltpu.make_async_copy(latent_ref, latent_out_ref, sem)
    copy.start()
    total = landed_ref[0].astype(F32)
    for number in range(1, landed_ref.shape[0]):
        total = total + landed_ref[number].astype(F32)
    mixed_ref[...] = total.astype(BF)
    copy.wait()


def last(landed, latent):
    anywhere = pl.BlockSpec(memory_space=pl.ANY)
    return pl.pallas_call(
        last_kernel,
        out_shape=(
            jax.ShapeDtypeStruct(landed.shape[1:], BF),
            jax.ShapeDtypeStruct(latent.shape, BF),
        ),
        in_specs=[VMEM, anywhere],
        out_specs=(VMEM, anywhere),
        scratch_shapes=[pltpu.SemaphoreType.DMA],
        compiler_params=PARAMS,
        name="last_sum",
    )(landed, latent)


def shards(
    tokens_a,
    norm_gain,
    expert_ids,
    route_weights,
    w_gate,
    w_up,
    w_down,
    queries_b,
    cache_b,
    lengths_b,
):
    x_size, z_size, cores = lax.axis_size("x"), lax.axis_size("z"), lax.axis_size("c")
    rows = tokens_a.shape[0]
    width = w_gate.shape[1]
    lanes = 128

    columns = w_down.shape[2] // 2
    half_shape = jax.ShapeDtypeStruct((w_down.shape[1], columns), BF)
    normed, mine, send = pl.pallas_call(
        norm_kernel,
        grid=(1,),
        out_shape=(
            jax.ShapeDtypeStruct((x_size, rows, width + lanes), BF), half_shape, half_shape
        ),
        in_specs=[
            pl.BlockSpec(shape, lambda i: (0, 0))
            for shape in (tokens_a.shape, (1, norm_gain.shape[0])) + 2 * (expert_ids.shape[::-1],)
            + (w_down.shape[1:],)
        ],
        out_specs=(VMEM, VMEM, VMEM),
        compiler_params=WIDE,
        name="norm_rows",
    )(tokens_a, norm_gain.reshape(1, -1), expert_ids.T, route_weights.T, w_down[0])
    sliced = lax.all_to_all(normed, "x", split_axis=0, concat_axis=0, tiled=True)
    gathered = lax.all_gather(
        sliced.reshape(x_size * rows, width + lanes), ("z", "c"), axis=0, tiled=True
    ).reshape(z_size, cores, x_size, rows, width + lanes)

    theirs = swap(send, "h")
    mine_lower, mine_upper = shift(mine, 1), shift(mine, -1)
    theirs_lower, theirs_upper = shift(theirs, 1), shift(theirs, -1)
    across = (shift(mine_lower, 1), shift(theirs_upper, -1))
    result, mine_upper = attention(queries_b, cache_b, lengths_b, mine_upper)
    weights = (mine, theirs, mine_lower, theirs_lower, mine_upper, theirs_upper, *across)

    latent_b = answer(result)
    gathered, latent_b, near = lax.optimization_barrier((gathered, latent_b, weights[:6]))
    core, x_place = lax.axis_index("c"), lax.axis_index("x")
    partial = gate_up(gathered, w_gate[0], w_up[0])
    partial, across = lax.optimization_barrier((partial, across))
    weights = (*near, *across)
    parts = lax.all_to_all(partial, "x", split_axis=0, concat_axis=0, tiled=True)
    active = swiglu(parts)
    active_other = swap(active, "h")
    place = jnp.stack([lax.rem(core + 1, cores), x_place])
    sent, kept = down(active, active_other, gathered, place, weights)
    out = (kept.astype(F32) + swap(sent, "c").astype(F32)).astype(BF)
    both = out.reshape(-1, rows, columns)
    landed = lax.all_to_all(both, ("k", "z"), split_axis=0, concat_axis=0, tiled=True)
    return last(landed, latent_b)


def solution(mesh):
    x_size, y_size, e_size = (mesh.shape[name] for name in ("dp", "tensor", "expert"))
    cores = 2
    fine = Mesh(
        mesh.devices.reshape(x_size, y_size // 2, 2, e_size // cores, cores),
        ("x", "k", "h", "z", "c"),
    )
    rows, tensor, expert = ("x", "z", "c"), ("k", "h"), ("z", "c")
    placed = (
        P(rows, None),
        P(),
        P(rows, None),
        P(rows, None),
        P(expert, "x", tensor),
        P(expert, "x", tensor),
        P(expert, tensor, "x"),
        P(rows, None, tensor, None),
        P(rows, tensor, None, None),
        P(rows, tensor),
    )
    return jax.shard_map(
        shards,
        mesh=fine,
        in_specs=placed,
        out_specs=(P(rows, tensor), P(rows, None, tensor, None)),
        check_vma=False,
    )
```
